128 devices in a mesh: prefix: 16 (over x_lo, y, core), blk: 8 (over x_hi, z).
Axes of the slice: x: 4 (x_hi: 2, x_lo: 2; x = x_hi * 2 + x_lo), y: 4, z: 4, core: 2. Of those that a mesh axis runs over, the one named last changes fastest.
Arguments:
- queries: bfloat16 [2048, 8192], P(('prefix', 'blk')), may hold values from -24 to 24
- row_prompt: int32 [2048], P(('prefix', 'blk')), may hold values from 0 to 15, as said below
- suffix_length: int32 [2048], P(('prefix', 'blk')), may hold values from 1 to 128, as said below
- result_slot: int32 [2048], P(('prefix', 'blk')), may hold values from 0 to 15, as said below
- prompt_keys: bfloat16 [16, 16384, 1024], P('prefix', 'blk'), may hold values from -3 to 3
- prompt_values: bfloat16 [16, 16384, 1024], P('prefix', 'blk'), may hold values from -6 to 6
- continuation_keys: bfloat16 [2048, 128, 1024], P(('prefix', 'blk')), may hold values from -12 to 12
- continuation_values: bfloat16 [2048, 128, 1024], P(('prefix', 'blk')), may hold values from -6 to 6
Outputs:
- output: bfloat16 [2048, 8192], P(('prefix', 'blk'))
The draws below stay inside these ranges and needn't reach their ends.
Inputs may be any that keep to these rules, and one draw needn't show every extreme that they name: `row_prompt`: within the rows of one device, at most 2 rows name the same prompt; for every index of blk, one prompt is named by exactly 2 rows of every device with that index. `suffix_length`: every device holds a row of length 128. `result_slot`: within the 16 rows of one device the values are a permutation of 0 to 15.
All inputs are finite; a program needn't handle non-finite values.
Results may differ from the reference program's by a relative error of at most 0.005.
Values may be sent and summed in bfloat16 or wider, within the bound.
No kernel may reach another device: no remote copies, remote signals or barrier semaphores. Data moves between devices by JAX's collectives and lax.ppermute only.
A program may use at most 128 MiB of HBM per device.

```python
import jax
import jax.numpy as jnp
from jax import lax

QUERY_HEADS = 64
KEY_HEADS = 8
HEAD_WIDTH = 128
HEADS_PER_KEY = 8
PROMPT_PER_CARD = 2048
ROWS_DEV = 16
CAP = 2
SUFFIX_LENGTH = 128
PROMPT_COUNT = 16
PROMPT_LENGTH = 16384
TOTAL_ROWS = 2048
N_BLK = 8


def route_table(key):
    base_level = jax.random.fold_in(key, 11)
    blocks = TOTAL_ROWS // ROWS_DEV
    pairs = PROMPT_COUNT * CAP
    tiers = jax.random.randint(jax.random.fold_in(base_level, 1), (PROMPT_COUNT,), 0, 4)
    noise_term = jax.random.randint(jax.random.fold_in(base_level, 2), (blocks, pairs), 0, 1 << 16)
    favored = jax.random.randint(jax.random.fold_in(base_level, 3), (N_BLK,), 0, PROMPT_COUNT)
    pair_prompt = jnp.arange(pairs) // CAP
    column_hot = favored[jnp.arange(blocks) % N_BLK]
    ranking = noise_term + tiers[pair_prompt][None, :] * (1 << 14)
    ranking = ranking + jnp.where(pair_prompt[None, :] == column_hot[:, None], 1 << 20, 0)
    ranking = ranking * pairs + jnp.arange(pairs)[None, :]
    _, chosen = lax.top_k(ranking, ROWS_DEV)
    shuffle = jax.random.randint(jax.random.fold_in(base_level, 4), (blocks, ROWS_DEV), 0, 1 << 16) * ROWS_DEV + jnp.arange(ROWS_DEV)[None, :]
    order = jnp.argsort(shuffle, axis=1)
    chosen = jnp.take_along_axis(chosen, order, axis=1)
    return (chosen // CAP).reshape(TOTAL_ROWS).astype(jnp.int32)


def length_table(key):
    private_key = jax.random.fold_in(key, 6)
    blocks = TOTAL_ROWS // ROWS_DEV
    length = jax.random.randint(private_key, (blocks, ROWS_DEV), 1, SUFFIX_LENGTH + 1)
    filled = jax.random.randint(jax.random.fold_in(private_key, 1), (blocks, 1), 0, ROWS_DEV)
    length = jnp.where(jnp.arange(ROWS_DEV)[None, :] == filled, SUFFIX_LENGTH, length)
    return length.reshape(TOTAL_ROWS).astype(jnp.int32)


def peak_spots(key):
    return jax.random.randint(jax.random.fold_in(key, 24), (PROMPT_COUNT,), 0, PROMPT_LENGTH - 1)


def prefix_rows(key, index, dispersion):
    base_level = jax.random.fold_in(key, 23)

    def one_key(token_position):
        return jax.random.uniform(jax.random.fold_in(base_level, token_position), (KEY_HEADS * HEAD_WIDTH,), jnp.float32, -dispersion, dispersion)
    return jax.vmap(one_key)(index)


def query_rows(key, dispersion, lift):
    prompts = route_table(key)
    coarse_estimate = jnp.clip(jax.random.normal(jax.random.fold_in(key, 21), (TOTAL_ROWS, QUERY_HEADS * HEAD_WIDTH), jnp.float32), -4.0, 4.0)
    intensity = jax.random.uniform(jax.random.fold_in(key, 22), (TOTAL_ROWS, 1), jnp.float32, 3.0, 8.0)
    spots = peak_spots(key)
    anchor_point = prefix_rows(key, prompts * PROMPT_LENGTH + spots[prompts], dispersion)
    lined_up = jnp.repeat(anchor_point.reshape(TOTAL_ROWS, KEY_HEADS, 1, HEAD_WIDTH), HEADS_PER_KEY, axis=2).reshape(TOTAL_ROWS, QUERY_HEADS * HEAD_WIDTH) * intensity
    picked = ((jnp.arange(TOTAL_ROWS) % 5 == 0) & (lift > 0.0))[:, None]
    return (coarse_estimate, jnp.where(picked, lined_up, coarse_estimate), anchor_point)


def draw_row_prompt(key, part):
    return route_table(key)


def draw_suffix_length(key, part):
    return length_table(key)


def draw_result_slot(key, part):
    private_key = jax.random.fold_in(key, 9)
    blocks = TOTAL_ROWS // ROWS_DEV
    shuffle = jax.random.randint(private_key, (blocks, ROWS_DEV), 0, 1 << 16) * ROWS_DEV + jnp.arange(ROWS_DEV)[None, :]
    return jnp.argsort(shuffle, axis=1).reshape(TOTAL_ROWS).astype(jnp.int32)


def draw_queries(key, part):
    dispersion = 1.7
    lift = 0.0
    coarse_estimate, final, anchor_point = query_rows(key, dispersion, lift)
    return final.astype(jnp.bfloat16)


def draw_prompt_keys(key, part):
    dispersion = 1.7
    twin = 0.0
    spots = peak_spots(key)
    index = jnp.arange(PROMPT_COUNT * PROMPT_LENGTH, dtype=jnp.int32)
    prompt = index // PROMPT_LENGTH
    token_position = index % PROMPT_LENGTH
    paired = (token_position == spots[prompt] + 1) & (twin > 0.0)
    sampled_rows = prefix_rows(key, jnp.where(paired, index - 1, index), dispersion)
    sampled_rows = sampled_rows * jnp.where(paired, 0.99, 1.0)[:, None]
    return sampled_rows.reshape(PROMPT_COUNT, PROMPT_LENGTH, KEY_HEADS * HEAD_WIDTH).astype(jnp.bfloat16)


def draw_continuation_keys(key, part):
    private_key = jax.random.fold_in(key, 4)
    dispersion = 1.7
    lift = 0.0
    coarse_estimate, final, anchor_point = query_rows(key, dispersion, lift)
    common_part = jnp.mean(coarse_estimate.reshape(TOTAL_ROWS, KEY_HEADS, HEADS_PER_KEY, HEAD_WIDTH), axis=2).reshape(TOTAL_ROWS, 1, KEY_HEADS * HEAD_WIDTH)
    noise_term = jnp.clip(jax.random.normal(private_key, (TOTAL_ROWS, SUFFIX_LENGTH, KEY_HEADS * HEAD_WIDTH), jnp.float32), -4.0, 4.0)
    drawn = noise_term + 2.0 * common_part
    lengths = length_table(key)
    token_position = jnp.arange(SUFFIX_LENGTH)
    picked = ((jnp.arange(TOTAL_ROWS) % 5 == 0) & (lift > 0.0))[:, None, None]
    last = jnp.maximum(lengths - 1, 0)[:, None]
    at_last = (token_position[None, :] == last)[:, :, None] & picked
    at_first = (token_position == 0)[None, :, None] & picked
    drawn = jnp.where(at_last, 0.988 * anchor_point[:, None, :], drawn)
    drawn = jnp.where(at_first, anchor_point[:, None, :], drawn)
    return drawn.astype(jnp.bfloat16)


def block_scale(rng, extent, split, smallest, largest):
    def one(position, blocks):
        heights = jax.random.uniform(jax.random.fold_in(jax.random.fold_in(rng, 6), position), (blocks,), jnp.float32, smallest / len(split), largest / len(split))
        return jnp.repeat(jnp.exp(heights), extent[position] // blocks).reshape((-1,) + (1,) * (len(extent) - position - 1))

    loudness = one(*split[0])
    for cut in split[1:]:
        loudness = loudness * one(*cut)
    return loudness


def noise(rng, extent, width, reach, shards=(), held_as=jnp.bfloat16):
    values = jax.random.normal(rng, extent, jnp.float32) * width
    if len(shards) > 0:
        values = block_scale(rng, extent, shards, -0.22, 0.18) * values
    return jnp.clip(values, min=-reach, max=reach).astype(held_as)


def setup_inputs(seed: int = 0) -> dict:
    key_list = jax.random.split(jax.random.key(seed), 9)
    return {
        "queries": draw_queries(jax.random.fold_in(key_list[8], 71), 0),
        "row_prompt": draw_row_prompt(jax.random.fold_in(key_list[8], 71), 0),
        "suffix_length": draw_suffix_length(jax.random.fold_in(key_list[8], 71), 0),
        "result_slot": draw_result_slot(jax.random.fold_in(key_list[8], 71), 0),
        "prompt_keys": draw_prompt_keys(jax.random.fold_in(key_list[8], 71), 0),
        "prompt_values": noise(key_list[5], (PROMPT_COUNT, PROMPT_LENGTH, KEY_HEADS * HEAD_WIDTH), 1.0, 6.0, ((0, 16), (1, 8))),
        "continuation_keys": draw_continuation_keys(jax.random.fold_in(key_list[8], 71), 0),
        "continuation_values": noise(key_list[7], (TOTAL_ROWS, SUFFIX_LENGTH, KEY_HEADS * HEAD_WIDTH), 1.0, 6.0, ((0, 128),)),
    }


def partial_softmax(query_head_rows, key_entries, value_entries, visible):
    scores = jnp.einsum("kgd,tkd->kgt", query_head_rows, key_entries) * (HEAD_WIDTH ** -0.5)
    scores = jnp.where(visible, scores, -jnp.inf)
    highest = jnp.max(scores, axis=-1)
    weights = jnp.where(visible, jnp.exp(scores - highest[..., None]), 0.0)
    weights = lax.optimization_barrier(weights.astype(jnp.bfloat16)).astype(jnp.float32)
    totals = jnp.sum(weights, axis=-1)
    blended = jnp.einsum("kgt,tkd->kgd", weights, value_entries)
    return highest, totals, blended


def reference(queries, row_prompt, suffix_length, result_slot, prompt_keys, prompt_values, continuation_keys, continuation_values):
    def one_row(packed):
        single_query, prompt, key_suffix_part, value_suffix_part, length = packed
        query_head_rows = single_query.astype(jnp.float32).reshape(KEY_HEADS, HEADS_PER_KEY, HEAD_WIDTH)
        key_entries = lax.dynamic_index_in_dim(prompt_keys, prompt, 0, keepdims=False)
        value_entries = lax.dynamic_index_in_dim(prompt_values, prompt, 0, keepdims=False)
        key_entries = key_entries.astype(jnp.float32).reshape(N_BLK, PROMPT_PER_CARD, KEY_HEADS, HEAD_WIDTH)
        value_entries = value_entries.astype(jnp.float32).reshape(N_BLK, PROMPT_PER_CARD, KEY_HEADS, HEAD_WIDTH)
        visible_all = jnp.ones((PROMPT_PER_CARD,), dtype=jnp.bool_)
        highest, totals, blended = jax.vmap(partial_softmax, in_axes=(None, 0, 0, None))(query_head_rows, key_entries, value_entries, visible_all)
        means = lax.optimization_barrier((blended / totals[..., None]).astype(jnp.bfloat16)).astype(jnp.float32)
        tail_visible = jnp.arange(SUFFIX_LENGTH) < length
        tail_high, tail_total, tail_blend = partial_softmax(
            query_head_rows,
            key_suffix_part.astype(jnp.float32).reshape(SUFFIX_LENGTH, KEY_HEADS, HEAD_WIDTH),
            value_suffix_part.astype(jnp.float32).reshape(SUFFIX_LENGTH, KEY_HEADS, HEAD_WIDTH),
            tail_visible)
        overall = jnp.maximum(jnp.max(highest, axis=0), tail_high)
        factor = jnp.exp(highest - overall)
        tail_factor = jnp.exp(tail_high - overall)
        numerator = jnp.sum((factor * totals)[..., None] * means, axis=0) + tail_factor[..., None] * tail_blend
        denominator = jnp.sum(factor * totals, axis=0) + tail_factor * tail_total
        return (numerator / denominator[..., None]).reshape(QUERY_HEADS * HEAD_WIDTH).astype(jnp.bfloat16)

    results = lax.map(one_row, (queries, row_prompt, continuation_keys, continuation_values, suffix_length))
    target_rows = (jnp.arange(TOTAL_ROWS, dtype=jnp.int32) // ROWS_DEV * ROWS_DEV + result_slot).astype(jnp.int32)
    return jnp.zeros((TOTAL_ROWS, QUERY_HEADS * HEAD_WIDTH), jnp.bfloat16).at[target_rows].set(results)
```

```python
import functools

import jax
import jax.numpy as jnp
from jax import lax
from jax.experimental import pallas as pl
from jax.experimental.pallas import tpu as pltpu
from jax.sharding import Mesh
from jax.sharding import PartitionSpec as P

KEY_HEADS = 8
HEAD_WIDTH = 128
HEADS_PER_KEY = 8
KEY_SPAN = HEADS_PER_KEY * HEAD_WIDTH
CAP = 2
Z = 4
GROUPS = 2
STAT = 32
SCALE = HEAD_WIDTH ** (-0.5) * 1.4426950408889634
MIB = 1024 * 1024
F32 = jnp.float32
BF16 = jnp.bfloat16


def params(mib):
    return pltpu.CompilerParams(vmem_limit_bytes=mib * MIB)


def lanes(shape):
    return lax.broadcasted_iota(jnp.int32, shape, len(shape) - 1)


def encode(stat):
    hi = stat.astype(BF16)
    rest = stat - hi.astype(F32)
    mid = rest.astype(BF16)
    lo = (rest - mid.astype(F32)).astype(BF16)
    lane = lanes(stat.shape)
    return jnp.where(
        lane < STAT, hi.astype(F32), jnp.where(lane < 2 * STAT, mid.astype(F32), lo.astype(F32))
    ).astype(BF16)


def decode(plane):
    plane = plane.astype(F32)
    return plane + pltpu.roll(plane, 128 - STAT, 1) + pltpu.roll(plane, 128 - 2 * STAT, 1)


def prefix_kernel(rows, many, *refs):
    q_refs, (k_ref, v_ref) = refs[:many], refs[many : many + 2]
    out_refs, wide, stat = refs[-2 - many : -2], refs[-2], refs[-1]
    step = pl.program_id(0)
    width = out_refs[0].shape[1] - 128

    @pl.when(step == 0)
    def _():
        wide[:, HEAD_WIDTH:] = jnp.ones((wide.shape[0], HEAD_WIDTH), BF16)
        stat[...] = jnp.zeros_like(stat)

    wide[:, :HEAD_WIDTH] = v_ref[...]
    per_tile = 256 // rows
    lane = lanes((rows, 128))
    tiles = [(i, h) for i in range(many) for h in range(0, HEADS_PER_KEY, per_tile)]
    gathered = [stat[i] for i in range(many)]

    def columns(h):
        return pl.ds(pl.multiple_of(step * KEY_SPAN + h * HEAD_WIDTH, HEAD_WIDTH), HEAD_WIDTH)

    def score(i, first):
        q = jnp.concatenate([q_refs[i][:, columns(first + j)] for j in range(per_tile)], axis=0)
        return lax.dot_general(
            q, k_ref[...], (((1,), (1,)), ((), ())), preferred_element_type=F32
        )

    scores = score(*tiles[0])
    waiting = None
    for n in range(len(tiles) + 1):
        ahead = score(*tiles[n + 1]) if n + 1 < len(tiles) else None
        if waiting is not None:
            both = jnp.dot(waiting[1], wide[...], preferred_element_type=F32)
        old = waiting
        if n < len(tiles):
            top = jnp.max(scores, axis=1, keepdims=True)
            waiting = (top, jnp.exp2((scores - top) * SCALE).astype(BF16))
        if old is not None:
            i, first = tiles[n - 1]
            total = both[:, HEAD_WIDTH:]
            mean = (both[:, :HEAD_WIDTH] / total).astype(BF16)
            level = old[0] * SCALE + jnp.log2(total)
            for j in range(per_tile):
                part = slice(j * rows, (j + 1) * rows)
                out_refs[i][:, columns(first + j)] = mean[part]
                here = lane % STAT == step * HEADS_PER_KEY + first + j
                gathered[i] = jnp.where(here, level[part], gathered[i])
        scores = ahead
    for i in range(many):
        stat[i] = gathered[i]

    @pl.when(step == pl.num_programs(0) - 1)
    def _():
        for i in range(many):
            out_refs[i][:, width:] = encode(gathered[i])


def prefix_part(queries, keys, values, group, after=()):
    many = len(queries)
    rows, width = queries[0].shape
    count = width // KEY_SPAN
    length = keys.shape[0]
    entry = pl.BlockSpec((length, HEAD_WIDTH), lambda k: (0, group * count + k))
    block = pl.BlockSpec((rows, width), lambda k: (0, 0))
    return pl.pallas_call(
        functools.partial(prefix_kernel, rows, many),
        grid=(count,),
        in_specs=[block] * many
        + [entry, entry]
        + [pl.BlockSpec(memory_space=pl.ANY)] * len(after),
        out_specs=[pl.BlockSpec((rows, width + 128), lambda k: (0, 0))] * many,
        out_shape=[jax.ShapeDtypeStruct((rows, width + 128), BF16)] * many,
        scratch_shapes=[
            pltpu.VMEM((length, 2 * HEAD_WIDTH), BF16),
            pltpu.VMEM((many, rows, 128), F32),
        ],
        compiler_params=params(40),
        cost_estimate=pl.CostEstimate(
            flops=8 * many * rows * width * length,
            bytes_accessed=4 * length * width // 8 + 4 * many * rows * width,
            transcendentals=many * rows * width // HEAD_WIDTH * length,
        ),
        name="prefix_attention",
    )(*queries, keys, values, *after)


def merged(stats, parts, count):
    top = functools.reduce(jnp.maximum, stats)
    weights = [jnp.exp2(s - top) for s in stats]
    total = functools.reduce(jnp.add, weights)
    shares = [w / total for w in weights]
    out = []
    for h in range(count):
        out.append(
            functools.reduce(jnp.add, [w[:, h : h + 1] * part(h) for w, part in zip(shares, parts)])
        )
    return out, top + jnp.log2(total)


def merge_kernel(*refs):
    ins, out_ref = refs[:-1], refs[-1]
    width = out_ref.shape[1] - 128
    stats = [decode(r[:, width:]) for r in ins]
    parts = [
        lambda h, r=r: r[:, h * HEAD_WIDTH : (h + 1) * HEAD_WIDTH].astype(F32) for r in ins
    ]
    out, stat = merged(stats, parts, width // HEAD_WIDTH)
    for h, x in enumerate(out):
        out_ref[:, h * HEAD_WIDTH : (h + 1) * HEAD_WIDTH] = x.astype(BF16)
    lane = lanes(stat.shape)
    stat = jnp.where(lane < STAT, stat, 0.0)
    stat = stat + pltpu.roll(stat, STAT, 1) + pltpu.roll(stat, 2 * STAT, 1)
    out_ref[:, width:] = encode(stat)


def merge(*messages):
    first = messages[0]
    return pl.pallas_call(
        merge_kernel,
        out_shape=jax.ShapeDtypeStruct(first.shape, BF16),
        compiler_params=params(24),
        cost_estimate=pl.CostEstimate(
            flops=first.size * 4, bytes_accessed=first.size * 2 * (len(messages) + 1), transcendentals=0
        ),
        name="merge_partials",
    )(*messages)


def outgoing_kernel(prompt_ref, q_ref, out_ref):
    rows, slots = q_ref.shape[0], out_ref.shape[0]
    prompt = prompt_ref[...]
    across = jnp.broadcast_to(prompt, (rows, rows))
    first = lax.broadcasted_iota(jnp.int32, (rows, rows), 0) < lanes((rows, rows))
    earlier = (across.T == across) & first
    arrival = jnp.sum(earlier.astype(jnp.int32), axis=0, keepdims=True)
    slot = lax.broadcasted_iota(jnp.int32, (slots, rows), 0)
    wanted = (slot // (2 * CAP) == prompt) & (slot % CAP == arrival)
    chooser = jnp.where(wanted, 1.0, 0.0).astype(BF16)
    out_ref[...] = jnp.dot(chooser, q_ref[...], preferred_element_type=F32).astype(BF16)


def outgoing_part(row_prompt, queries, slots):
    rows, width = queries.shape
    whole = lambda shape: pl.BlockSpec(shape, lambda i: (0, i))
    return pl.pallas_call(
        outgoing_kernel,
        grid=(4,),
        in_specs=[pl.BlockSpec((1, rows), lambda i: (0, 0)), whole((rows, width // 4))],
        out_specs=whole((slots, width // 4)),
        out_shape=jax.ShapeDtypeStruct((slots, width), BF16),
        compiler_params=params(16),
        name="outgoing_queries",
    )(row_prompt[None, :], queries)


def suffix_kernel(length_ref, slot_ref, q_ref, k_ref, v_ref, mean_ref, stat_ref):
    heads = KEY_HEADS * HEADS_PER_KEY
    rows = q_ref.shape[0]
    shape = (heads, KEY_HEADS * HEAD_WIDTH)
    mine = lanes(shape) // HEAD_WIDTH == lax.broadcasted_iota(jnp.int32, shape, 0) // HEADS_PER_KEY
    square = lanes((heads, 128)) == lax.broadcasted_iota(jnp.int32, (heads, 128), 0)
    for i in range(rows):
        row = pl.program_id(0) * rows + i
        slot = slot_ref[row]
        q = jnp.concatenate([q_ref[i]] * KEY_HEADS, axis=1)
        q = jnp.where(mine, q, jnp.zeros_like(q))
        scores = lax.dot_general(
            q, k_ref[i], (((1,), (1,)), ((), ())), preferred_element_type=F32
        )
        seen = lanes(scores.shape) < length_ref[row]
        scores = jnp.where(seen, scores * SCALE, -jnp.inf)
        top = jnp.max(scores, axis=1, keepdims=True)
        weights = jnp.exp2(scores - top).astype(BF16)
        total = jnp.sum(weights.astype(F32), axis=1, keepdims=True)
        blend = jnp.dot(weights, v_ref[i], preferred_element_type=F32)
        for k in range(KEY_HEADS):
            part = slice(k * HEADS_PER_KEY, (k + 1) * HEADS_PER_KEY)
            mean_ref[slot, part, :] = (
                blend[part, k * HEAD_WIDTH : (k + 1) * HEAD_WIDTH] / total[part]
            )
        level = top + jnp.log2(total)
        stat_ref[slot] = jnp.sum(jnp.where(square, level, 0.0), axis=0, keepdims=True)


def suffix_part(queries, keys, values, length, slot, step=4):
    rows, width = queries.shape
    heads = width // HEAD_WIDTH
    entry = pl.BlockSpec((step,) + keys.shape[1:], lambda r, *_: (r, 0, 0))
    return pl.pallas_call(
        suffix_kernel,
        grid_spec=pltpu.PrefetchScalarGridSpec(
            num_scalar_prefetch=2,
            grid=(rows // step,),
            in_specs=[
                pl.BlockSpec((step, heads, HEAD_WIDTH), lambda r, *_: (r, 0, 0)),
                entry,
                entry,
            ],
            out_specs=[
                pl.BlockSpec((rows, heads, HEAD_WIDTH), lambda r, *_: (0, 0, 0)),
                pl.BlockSpec((rows, 1, 128), lambda r, *_: (0, 0, 0)),
            ],
        ),
        out_shape=[
            jax.ShapeDtypeStruct((rows, heads, HEAD_WIDTH), F32),
            jax.ShapeDtypeStruct((rows, 1, 128), F32),
        ],
        compiler_params=params(58),
        cost_estimate=pl.CostEstimate(
            flops=2 * keys.size * heads * 2,
            bytes_accessed=keys.size * 4,
            transcendentals=rows * heads * keys.shape[1],
        ),
        name="suffix_attention",
    )(length, slot, queries.reshape(rows, heads, HEAD_WIDTH), keys, values)


def final_kernel(*refs):
    arrived, (pick_ref, mean_ref, stat_ref, out_ref) = refs[:-4], refs[-4:]
    for group, ref in enumerate(arrived):
        width = ref.shape[1] - 128
        count = width // HEAD_WIDTH
        stats, parts = [], []
        for half in range(2):
            chosen = jnp.dot(pick_ref[half], ref[...], preferred_element_type=F32)
            stats.append(decode(chosen[:, width:]))
            parts.append(lambda h, c=chosen: c[:, h * HEAD_WIDTH : (h + 1) * HEAD_WIDTH])
        base = group * width
        stat = stat_ref[:, 0, :]
        if group:
            stat = pltpu.roll(stat, 128 - group * count, 1)
        stats.append(stat)
        parts.append(
            lambda h: mean_ref[:, group * count + h, :]
        )
        out, _ = merged(stats, parts, count)
        for h, x in enumerate(out):
            out_ref[:, base + h * HEAD_WIDTH : base + (h + 1) * HEAD_WIDTH] = x.astype(BF16)


def final_part(arrived, pick, mean, stat):
    return pl.pallas_call(
        final_kernel,
        out_shape=jax.ShapeDtypeStruct((mean.shape[0], mean.shape[1] * mean.shape[2]), BF16),
        compiler_params=params(24),
        name="last_merge",
    )(*arrived, pick, mean, stat)


def swapped(x, turn):
    pairs = {"near": [1, 0, 3, 2], "next": [3, 2, 1, 0], "far": [2, 3, 0, 1]}[turn]
    return lax.ppermute(x, "z", list(enumerate(pairs)))


def later(x, after):
    return lax.optimization_barrier((x, after))[0]


def in_plane(x):
    return lax.all_to_all(x, ("prefix", "xh"), split_axis=0, concat_axis=0, tiled=True)


def local(
    queries,
    row_prompt,
    suffix_length,
    result_slot,
    prompt_keys,
    prompt_values,
    continuation_keys,
    continuation_values,
):
    sides = lax.axis_size("xh")
    rows = queries.shape[0]
    slots = lax.axis_size("prefix") * sides * CAP
    whole = in_plane(outgoing_part(row_prompt, queries, slots))
    mean, stat = suffix_part(
        queries, continuation_keys, continuation_values, suffix_length, result_slot
    )
    span = queries.shape[1] // GROUPS
    arrived = [whole[:, g * span : (g + 1) * span] for g in range(GROUPS)]
    indices = jnp.arange(rows)
    earlier = (row_prompt[:, None] == row_prompt[None, :]) & (indices[None, :] < indices[:, None])
    arrival = jnp.sum(earlier.astype(jnp.int32), axis=1)
    slot = jnp.arange(slots)
    wanted = (slot[None, :] // (sides * CAP) == row_prompt[:, None]) & (
        slot[None, :] % CAP == arrival[:, None]
    )
    placer = indices[:, None] == result_slot[None, :]
    taken = jnp.any(placer[:, :, None] & wanted[None], axis=1)
    side = slot // CAP % sides
    pick = jnp.stack([taken & (side == x)[None] for x in range(2)]).astype(BF16)
    keys, values = prompt_keys[0], prompt_values[0]
    attend = lambda group, queries, after: prefix_part(queries, keys, values, group, after)
    near_0, next_0 = swapped(arrived[0], "near"), swapped(arrived[0], "next")
    own_0 = attend(0, [arrived[0]], [stat])
    far_q_0 = swapped(later(arrived[0], own_0), "far")
    own_1 = attend(1, [arrived[1]], own_0)
    source_1 = later(arrived[1], own_1)
    near_1, next_1 = swapped(source_1, "near"), swapped(source_1, "next")
    pair_0 = attend(0, [near_0, next_0], own_1)
    far_q_1 = swapped(later(arrived[1], pair_0), "far")
    back_0 = [swapped(pair_0[0], "near"), swapped(pair_0[1], "next")]
    far_0 = attend(0, [far_q_0], pair_0[:1])
    back_0.append(swapped(far_0[0], "far"))
    pair_1 = attend(1, [near_1, next_1], far_0)
    back_1 = [swapped(pair_1[0], "near"), swapped(pair_1[1], "next")]
    far_1 = attend(1, [far_q_1], pair_1[:1])
    back_1.append(swapped(far_1[0], "far"))
    back_0 = later(back_0, far_1)
    returned = [
        in_plane(merge(own_0[0], *back_0)),
        in_plane(merge(own_1[0], *back_1)),
    ]
    return final_part(returned, pick, mean, stat)


def solution(mesh):
    fine = Mesh(mesh.devices.reshape(mesh.devices.shape[0], -1, Z), ("prefix", "xh", "z"))
    rows = ("prefix", "xh", "z")
    blocks = ("xh", "z")
    in_specs = (
        P(rows, None),
        P(rows),
        P(rows),
        P(rows),
        P("prefix", blocks, None),
        P("prefix", blocks, None),
        P(rows, None, None),
        P(rows, None, None),
    )
    return jax.shard_map(
        local, mesh=fine, in_specs=in_specs, out_specs=P(rows, None), check_vma=False
    )
```

```python
import functools

import jax
import jax.numpy as jnp
from jax import lax
from jax.experimental import pallas as pl
from jax.experimental.pallas import tpu as pltpu
from jax.sharding import Mesh
from jax.sharding import PartitionSpec as P

KEY_HEADS = 8
HEAD_WIDTH = 128
HEADS_PER_KEY = 8
KEY_SPAN = HEADS_PER_KEY * HEAD_WIDTH
CAP = 2
Z = 4
GROUPS = 2
STAT = 32
SCALE = HEAD_WIDTH ** (-0.5) * 1.4426950408889634
MIB = 1024 * 1024
TUNE = 0.5
F32 = jnp.float32
BF16 = jnp.bfloat16


def cost(us):
    return pl.CostEstimate(flops=int(us * 1.15e9), bytes_accessed=0, transcendentals=0)


def params(mib):
    return pltpu.CompilerParams(vmem_limit_bytes=mib * MIB)


def lanes(shape):
    return lax.broadcasted_iota(jnp.int32, shape, len(shape) - 1)


def encode(stat):
    hi = stat.astype(BF16)
    rest = stat - hi.astype(F32)
    mid = rest.astype(BF16)
    lo = (rest - mid.astype(F32)).astype(BF16)
    lane = lanes(stat.shape)
    return jnp.where(
        lane < STAT, hi.astype(F32), jnp.where(lane < 2 * STAT, mid.astype(F32), lo.astype(F32))
    ).astype(BF16)


def decode(plane):
    plane = plane.astype(F32)
    return plane + pltpu.roll(plane, 128 - STAT, 1) + pltpu.roll(plane, 128 - 2 * STAT, 1)


def prefix_kernel(rows, many, split, *refs):
    q_refs, (k_ref, v_ref) = refs[: 2 * many], refs[2 * many : 2 * many + 2]
    out_refs, wide, stat = refs[-2 - many * split : -2], refs[-2], refs[-1]
    share = rows // split
    step = pl.program_id(0)
    width = out_refs[0].shape[1] - 128

    @pl.when(step == 0)
    def _():
        wide[:, HEAD_WIDTH:] = jnp.ones((wide.shape[0], HEAD_WIDTH), BF16)
        stat[...] = jnp.zeros_like(stat)

    wide[:, :HEAD_WIDTH] = v_ref[...]
    per_tile = 256 // rows
    lane = lanes((rows, 128))
    tiles = [(i, h) for i in range(many) for h in range(0, HEADS_PER_KEY, per_tile)]
    gathered = [stat[i] for i in range(many)]

    def columns(h):
        return pl.ds(pl.multiple_of(step * KEY_SPAN + h * HEAD_WIDTH, HEAD_WIDTH), HEAD_WIDTH)

    def score(i, first):
        q = jnp.concatenate(
            [r[:, columns(first + j)] for j in range(per_tile) for r in q_refs[2 * i : 2 * i + 2]],
            axis=0,
        )
        return lax.dot_general(
            q, k_ref[...], (((1,), (1,)), ((), ())), preferred_element_type=F32
        )

    scores = score(*tiles[0])
    waiting = None
    for n in range(len(tiles) + 1):
        ahead = score(*tiles[n + 1]) if n + 1 < len(tiles) else None
        if waiting is not None:
            both = jnp.dot(waiting[1], wide[...], preferred_element_type=F32)
        old = waiting
        if n < len(tiles):
            top = jnp.max(scores, axis=1, keepdims=True)
            waiting = (top, jnp.exp2((scores - top) * SCALE).astype(BF16))
        if old is not None:
            i, first = tiles[n - 1]
            total = both[:, HEAD_WIDTH:]
            mean = (both[:, :HEAD_WIDTH] / total).astype(BF16)
            level = old[0] * SCALE + jnp.log2(total)
            for j in range(per_tile):
                part = slice(j * rows, (j + 1) * rows)
                for n_out in range(split):
                    rest = j * rows + n_out * share
                    out_refs[i * split + n_out][:, columns(first + j)] = mean[rest : rest + share]
                here = lane % STAT == step * HEADS_PER_KEY + first + j
                gathered[i] = jnp.where(here, level[part], gathered[i])
        scores = ahead
    for i in range(many):
        stat[i] = gathered[i]

    @pl.when(step == pl.num_programs(0) - 1)
    def _():
        for i in range(many * split):
            rest = i % split * share
            out_refs[i][:, width:] = encode(gathered[i // split][rest : rest + share])


def prefix_part(queries, keys, values, group, after=(), split=1):
    many = len(queries)
    queries = [half for block in queries for half in block]
    rows, width = 2 * queries[0].shape[0], queries[0].shape[1]
    count = width // KEY_SPAN
    length = keys.shape[0]
    entry = pl.BlockSpec((length, HEAD_WIDTH), lambda k: (0, group * count + k))
    block = pl.BlockSpec((rows // 2, width), lambda k: (0, 0))
    return pl.pallas_call(
        functools.partial(prefix_kernel, rows, many, split),
        grid=(count,),
        in_specs=[block] * len(queries)
        + [entry, entry]
        + [pl.BlockSpec(memory_space=pl.ANY)] * len(after),
        out_specs=[pl.BlockSpec((rows // split, width + 128), lambda k: (0, 0))] * (many * split),
        out_shape=[jax.ShapeDtypeStruct((rows // split, width + 128), BF16)] * (many * split),
        scratch_shapes=[
            pltpu.VMEM((length, 2 * HEAD_WIDTH), BF16),
            pltpu.VMEM((many, rows, 128), F32),
        ],
        compiler_params=params(40),
        cost_estimate=cost((1 + 6 * many) * TUNE),
        name="prefix_attention",
    )(*queries, keys, values, *after)


def merged(stats, parts, count):
    top = functools.reduce(jnp.maximum, stats)
    weights = [jnp.exp2(s - top) for s in stats]
    total = functools.reduce(jnp.add, weights)
    shares = [w / total for w in weights]
    out = []
    for h in range(count):
        out.append(
            functools.reduce(jnp.add, [w[:, h : h + 1] * part(h) for w, part in zip(shares, parts)])
        )
    return out, top + jnp.log2(total)


def merge_kernel(many, *refs):
    ins, out_ref = refs[:many], refs[-1]
    width = out_ref.shape[1] - 128
    stats = [decode(r[:, width:]) for r in ins]
    parts = [
        lambda h, r=r: r[:, h * HEAD_WIDTH : (h + 1) * HEAD_WIDTH].astype(F32) for r in ins
    ]
    out, stat = merged(stats, parts, width // HEAD_WIDTH)
    for h, x in enumerate(out):
        out_ref[:, h * HEAD_WIDTH : (h + 1) * HEAD_WIDTH] = x.astype(BF16)
    lane = lanes(stat.shape)
    stat = jnp.where(lane < STAT, stat, 0.0)
    stat = stat + pltpu.roll(stat, STAT, 1) + pltpu.roll(stat, 2 * STAT, 1)
    out_ref[:, width:] = encode(stat)


def merge(messages, after=()):
    first = messages[0]
    return pl.pallas_call(
        functools.partial(merge_kernel, len(messages)),
        in_specs=[pl.BlockSpec(memory_space=pltpu.VMEM)] * len(messages)
        + [pl.BlockSpec(memory_space=pl.ANY)] * len(after),
        out_shape=jax.ShapeDtypeStruct(first.shape, BF16),
        compiler_params=params(24),
        cost_estimate=cost(1 * TUNE),
        name="merge_partials",
    )(*messages, *after)


def fold_kernel(start, whole_ref, part_ref, out_ref):
    rows = part_ref.shape[0]
    rest = slice(rows - start, 2 * rows - start)
    out_ref[rest] = whole_ref[rest]
    here = slice(start, start + rows)
    merge_kernel(2, whole_ref.at[here], part_ref, out_ref.at[here])


def fold(whole, part, start):
    return pl.pallas_call(
        functools.partial(fold_kernel, start),
        out_shape=jax.ShapeDtypeStruct(whole.shape, BF16),
        compiler_params=params(24),
        cost_estimate=cost(0.1 * TUNE),
        name="fold_partials",
    )(whole, part)


def outgoing_kernel(prompt_ref, q_ref, out_ref):
    rows, slots = q_ref.shape[0], out_ref.shape[0]
    prompt = prompt_ref[...]
    across = jnp.broadcast_to(prompt, (rows, rows))
    first = lax.broadcasted_iota(jnp.int32, (rows, rows), 0) < lanes((rows, rows))
    earlier = (across.T == across) & first
    arrival = jnp.sum(earlier.astype(jnp.int32), axis=0, keepdims=True)
    slot = lax.broadcasted_iota(jnp.int32, (slots, rows), 0)
    wanted = (slot // (2 * CAP) == prompt) & (slot % CAP == arrival)
    chooser = jnp.where(wanted, 1.0, 0.0).astype(BF16)
    out_ref[...] = jnp.dot(chooser, q_ref[...], preferred_element_type=F32).astype(BF16)


def outgoing_part(row_prompt, queries, slots):
    rows, width = queries.shape
    whole = lambda shape: pl.BlockSpec(shape, lambda i: (0, i))
    return pl.pallas_call(
        outgoing_kernel,
        grid=(4,),
        in_specs=[pl.BlockSpec((1, rows), lambda i: (0, 0)), whole((rows, width // 4))],
        out_specs=whole((slots, width // 4)),
        out_shape=jax.ShapeDtypeStruct((slots, width), BF16),
        compiler_params=params(16),
        name="outgoing_queries",
    )(row_prompt[None, :], queries)


def suffix_kernel(length_ref, slot_ref, q_ref, k_ref, v_ref, mean_ref, stat_ref):
    heads = KEY_HEADS * HEADS_PER_KEY
    rows = q_ref.shape[0]
    shape = (heads, KEY_HEADS * HEAD_WIDTH)
    mine = lanes(shape) // HEAD_WIDTH == lax.broadcasted_iota(jnp.int32, shape, 0) // HEADS_PER_KEY
    square = lanes((heads, 128)) == lax.broadcasted_iota(jnp.int32, (heads, 128), 0)
    for i in range(rows):
        row = pl.program_id(0) * rows + i
        slot = slot_ref[row]
        q = jnp.concatenate([q_ref[i]] * KEY_HEADS, axis=1)
        q = jnp.where(mine, q, jnp.zeros_like(q))
        scores = lax.dot_general(
            q, k_ref[i], (((1,), (1,)), ((), ())), preferred_element_type=F32
        )
        seen = lanes(scores.shape) < length_ref[row]
        scores = jnp.where(seen, scores * SCALE, -jnp.inf)
        top = jnp.max(scores, axis=1, keepdims=True)
        weights = jnp.exp2(scores - top).astype(BF16)
        total = jnp.sum(weights.astype(F32), axis=1, keepdims=True)
        blend = jnp.dot(weights, v_ref[i], preferred_element_type=F32)
        for k in range(KEY_HEADS):
            part = slice(k * HEADS_PER_KEY, (k + 1) * HEADS_PER_KEY)
            mean_ref[slot, part, :] = (
                blend[part, k * HEAD_WIDTH : (k + 1) * HEAD_WIDTH] / total[part]
            )
        level = top + jnp.log2(total)
        stat_ref[slot] = jnp.sum(jnp.where(square, level, 0.0), axis=0, keepdims=True)


def suffix_part(queries, keys, values, length, slot, step=4):
    rows, width = queries.shape
    heads = width // HEAD_WIDTH
    entry = pl.BlockSpec((step,) + keys.shape[1:], lambda r, *_: (r, 0, 0))
    return pl.pallas_call(
        suffix_kernel,
        grid_spec=pltpu.PrefetchScalarGridSpec(
            num_scalar_prefetch=2,
            grid=(rows // step,),
            in_specs=[
                pl.BlockSpec((step, heads, HEAD_WIDTH), lambda r, *_: (r, 0, 0)),
                entry,
                entry,
            ],
            out_specs=[
                pl.BlockSpec((rows, heads, HEAD_WIDTH), lambda r, *_: (0, 0, 0)),
                pl.BlockSpec((rows, 1, 128), lambda r, *_: (0, 0, 0)),
            ],
        ),
        out_shape=[
            jax.ShapeDtypeStruct((rows, heads, HEAD_WIDTH), F32),
            jax.ShapeDtypeStruct((rows, 1, 128), F32),
        ],
        compiler_params=params(58),
        cost_estimate=cost(10),
        name="suffix_attention",
    )(length, slot, queries.reshape(rows, heads, HEAD_WIDTH), keys, values)


def final_kernel(*refs):
    arrived, (pick_ref, mean_ref, stat_ref, out_ref) = refs[:-4], refs[-4:]
    for group, ref in enumerate(arrived):
        width = ref.shape[1] - 128
        count = width // HEAD_WIDTH
        stats, parts = [], []
        for half in range(2):
            chosen = jnp.dot(pick_ref[half], ref[...], preferred_element_type=F32)
            stats.append(decode(chosen[:, width:]))
            parts.append(lambda h, c=chosen: c[:, h * HEAD_WIDTH : (h + 1) * HEAD_WIDTH])
        base = group * width
        stat = stat_ref[:, 0, :]
        if group:
            stat = pltpu.roll(stat, 128 - group * count, 1)
        stats.append(stat)
        parts.append(
            lambda h: mean_ref[:, group * count + h, :]
        )
        out, _ = merged(stats, parts, count)
        for h, x in enumerate(out):
            out_ref[:, base + h * HEAD_WIDTH : base + (h + 1) * HEAD_WIDTH] = x.astype(BF16)


def final_part(arrived, pick, mean, stat):
    return pl.pallas_call(
        final_kernel,
        out_shape=jax.ShapeDtypeStruct((mean.shape[0], mean.shape[1] * mean.shape[2]), BF16),
        compiler_params=params(24),
        name="last_merge",
    )(*arrived, pick, mean, stat)


def swapped(x, turn):
    pairs = {"near": [1, 0, 3, 2], "next": [3, 2, 1, 0], "far": [2, 3, 0, 1]}[turn]
    return lax.ppermute(x, "z", list(enumerate(pairs)))


def in_plane(x):
    return lax.all_to_all(x, ("prefix", "xh"), split_axis=0, concat_axis=0, tiled=True)


def local(
    queries,
    row_prompt,
    suffix_length,
    result_slot,
    prompt_keys,
    prompt_values,
    continuation_keys,
    continuation_values,
):
    sides = lax.axis_size("xh")
    rows = queries.shape[0]
    slots = lax.axis_size("prefix") * sides * CAP
    whole = in_plane(outgoing_part(row_prompt, queries, slots))
    mean, stat = suffix_part(
        queries, continuation_keys, continuation_values, suffix_length, result_slot
    )
    indices = jnp.arange(rows)
    earlier = (row_prompt[:, None] == row_prompt[None, :]) & (indices[None, :] < indices[:, None])
    arrival = jnp.sum(earlier.astype(jnp.int32), axis=1)
    slot = jnp.arange(slots)
    wanted = (slot[None, :] // (sides * CAP) == row_prompt[:, None]) & (
        slot[None, :] % CAP == arrival[:, None]
    )
    placer = indices[:, None] == result_slot[None, :]
    taken = jnp.any(placer[:, :, None] & wanted[None], axis=1)
    side = slot // CAP % sides
    pick = jnp.stack([taken & (side == x)[None] for x in range(2)]).astype(BF16)
    keys, values = prompt_keys[0], prompt_values[0]
    attend = lambda group, queries, after, split=1: prefix_part(
        queries, keys, values, group, after, split
    )
    half, span = slots // 2, queries.shape[1] // GROUPS
    own = [
        [whole[h * half : (h + 1) * half, g * span : (g + 1) * span] for h in range(2)]
        for g in range(GROUPS)
    ]
    near = [[swapped(x, "near") for x in block] for block in own]
    after = [[swapped(x, "next") for x in block] for block in own]
    far = [[swapped(a[0], "near"), swapped(n[1], "next")] for n, a in zip(near, after)]

    def folded(pair, far):
        top, low = swapped(far[0], "near"), swapped(far[1], "next")
        return fold(pair[0], low, half), fold(pair[1], top, 0)

    def back(sent):
        return swapped(sent[0], "near"), swapped(sent[1], "next")

    (own_0,) = attend(0, [own[0]], [stat])
    pair_0 = attend(0, [near[0], after[0]], [own_0])
    far_0 = attend(0, [far[0]], pair_0, 2)
    far_1 = attend(1, [far[1]], far_0, 2)
    sent_0 = folded(pair_0, far_0)
    pair_1 = attend(1, [near[1], after[1]], [*far_1, *sent_0])
    sent_1 = folded(pair_1, far_1)
    (own_1,) = attend(1, [own[1]], sent_1)
    first = in_plane(merge([own_0, *back(sent_0)], pair_1))
    second = in_plane(merge([own_1, *back(sent_1)], [first]))
    returned = [first, second]
    return final_part(returned, pick, mean, stat)


def solution(mesh):
    fine = Mesh(mesh.devices.reshape(mesh.devices.shape[0], -1, Z), ("prefix", "xh", "z"))
    rows = ("prefix", "xh", "z")
    blocks = ("xh", "z")
    in_specs = (
        P(rows, None),
        P(rows),
        P(rows),
        P(rows),
        P("prefix", blocks, None),
        P("prefix", blocks, None),
        P(rows, None, None),
        P(rows, None, None),
    )
    return jax.shard_map(
        local, mesh=fine, in_specs=in_specs, out_specs=P(rows, None), check_vma=False
    )
```

```python
import functools

import jax
import jax.numpy as jnp
from jax import lax
from jax.experimental import pallas as pl
from jax.experimental.pallas import tpu as pltpu
from jax.sharding import Mesh
from jax.sharding import PartitionSpec as P

KEY_HEADS = 8
HEAD_WIDTH = 128
HEADS_PER_KEY = 8
KEY_SPAN = HEADS_PER_KEY * HEAD_WIDTH
CAP = 2
Z = 4
GROUPS = 2
STAT = 32
SCALE = HEAD_WIDTH ** (-0.5) * 1.4426950408889634
MIB = 1024 * 1024
TUNE = 0.5
F32 = jnp.float32
BF16 = jnp.bfloat16


def cost(us):
    return pl.CostEstimate(flops=int(us * 1.15e9), bytes_accessed=0, transcendentals=0)


def params(mib):
    return pltpu.CompilerParams(vmem_limit_bytes=mib * MIB)


def lanes(shape):
    return lax.broadcasted_iota(jnp.int32, shape, len(shape) - 1)


def encode(stat):
    hi = stat.astype(BF16)
    rest = stat - hi.astype(F32)
    mid = rest.astype(BF16)
    lo = (rest - mid.astype(F32)).astype(BF16)
    lane = lanes(stat.shape)
    return jnp.where(
        lane < STAT, hi.astype(F32), jnp.where(lane < 2 * STAT, mid.astype(F32), lo.astype(F32))
    ).astype(BF16)


def decode(plane):
    plane = plane.astype(F32)
    return plane + pltpu.roll(plane, 128 - STAT, 1) + pltpu.roll(plane, 128 - 2 * STAT, 1)


def prefix_kernel(rows, many, split, *refs):
    q_refs, (k_ref, v_ref) = refs[: 2 * many], refs[2 * many : 2 * many + 2]
    out_refs, wide, stat = refs[-2 - many * split : -2], refs[-2], refs[-1]
    share = rows // split
    step = pl.program_id(0)
    width = out_refs[0].shape[1] - 128

    @pl.when(step == 0)
    def _():
        wide[:, HEAD_WIDTH:] = jnp.ones((wide.shape[0], HEAD_WIDTH), BF16)
        stat[...] = jnp.zeros_like(stat)

    wide[:, :HEAD_WIDTH] = v_ref[...]
    per_tile = 256 // rows
    lane = lanes((rows, 128))
    tiles = [(i, h) for i in range(many) for h in range(0, HEADS_PER_KEY, per_tile)]
    gathered = [stat[i] for i in range(many)]

    def columns(h):
        return pl.ds(pl.multiple_of(step * KEY_SPAN + h * HEAD_WIDTH, HEAD_WIDTH), HEAD_WIDTH)

    def score(i, first):
        q = jnp.concatenate(
            [r[:, columns(first + j)] for j in range(per_tile) for r in q_refs[2 * i : 2 * i + 2]],
            axis=0,
        )
        return lax.dot_general(
            q, k_ref[...], (((1,), (1,)), ((), ())), preferred_element_type=F32
        )

    scores = score(*tiles[0])
    waiting = None
    for n in range(len(tiles) + 1):
        ahead = score(*tiles[n + 1]) if n + 1 < len(tiles) else None
        if waiting is not None:
            both = jnp.dot(waiting[1], wide[...], preferred_element_type=F32)
        old = waiting
        if n < len(tiles):
            top = jnp.max(scores, axis=1, keepdims=True)
            waiting = (top, jnp.exp2((scores - top) * SCALE).astype(BF16))
        if old is not None:
            i, first = tiles[n - 1]
            total = both[:, HEAD_WIDTH:]
            mean = (both[:, :HEAD_WIDTH] / total).astype(BF16)
            level = old[0] * SCALE + jnp.log2(total)
            for j in range(per_tile):
                part = slice(j * rows, (j + 1) * rows)
                for n_out in range(split):
                    rest = j * rows + n_out * share
                    out_refs[i * split + n_out][:, columns(first + j)] = mean[rest : rest + share]
                here = lane % STAT == step * HEADS_PER_KEY + first + j
                gathered[i] = jnp.where(here, level[part], gathered[i])
        scores = ahead
    for i in range(many):
        stat[i] = gathered[i]

    @pl.when(step == pl.num_programs(0) - 1)
    def _():
        for i in range(many * split):
            rest = i % split * share
            out_refs[i][:, width:] = encode(gathered[i // split][rest : rest + share])


def prefix_part(queries, keys, values, group, after=(), split=1):
    many = len(queries)
    queries = [half for block in queries for half in block]
    rows, width = 2 * queries[0].shape[0], queries[0].shape[1]
    count = width // KEY_SPAN
    length = keys.shape[0]
    entry = pl.BlockSpec((length, HEAD_WIDTH), lambda k: (0, group * count + k))
    block = pl.BlockSpec((rows // 2, width), lambda k: (0, 0))
    return pl.pallas_call(
        functools.partial(prefix_kernel, rows, many, split),
        grid=(count,),
        in_specs=[block] * len(queries)
        + [entry, entry]
        + [pl.BlockSpec(memory_space=pl.ANY)] * len(after),
        out_specs=[pl.BlockSpec((rows // split, width + 128), lambda k: (0, 0))] * (many * split),
        out_shape=[jax.ShapeDtypeStruct((rows // split, width + 128), BF16)] * (many * split),
        scratch_shapes=[
            pltpu.VMEM((length, 2 * HEAD_WIDTH), BF16),
            pltpu.VMEM((many, rows, 128), F32),
        ],
        compiler_params=params(40),
        cost_estimate=cost((1 + 6 * many) * TUNE),
        name="prefix_attention",
    )(*queries, keys, values, *after)


def merged(stats, parts, count):
    top = functools.reduce(jnp.maximum, stats)
    weights = [jnp.exp2(s - top) for s in stats]
    total = functools.reduce(jnp.add, weights)
    shares = [w / total for w in weights]
    out = []
    for h in range(count):
        out.append(
            functools.reduce(jnp.add, [w[:, h : h + 1] * part(h) for w, part in zip(shares, parts)])
        )
    return out, top + jnp.log2(total)


def merge_kernel(many, *refs):
    ins, out_ref = refs[:many], refs[-1]
    width = out_ref.shape[1] - 128
    stats = [decode(r[:, width:]) for r in ins]
    parts = [
        lambda h, r=r: r[:, h * HEAD_WIDTH : (h + 1) * HEAD_WIDTH].astype(F32) for r in ins
    ]
    out, stat = merged(stats, parts, width // HEAD_WIDTH)
    for h, x in enumerate(out):
        out_ref[:, h * HEAD_WIDTH : (h + 1) * HEAD_WIDTH] = x.astype(BF16)
    lane = lanes(stat.shape)
    stat = jnp.where(lane < STAT, stat, 0.0)
    stat = stat + pltpu.roll(stat, STAT, 1) + pltpu.roll(stat, 2 * STAT, 1)
    out_ref[:, width:] = encode(stat)


def merge(messages, after=()):
    first = messages[0]
    return pl.pallas_call(
        functools.partial(merge_kernel, len(messages)),
        in_specs=[pl.BlockSpec(memory_space=pltpu.VMEM)] * len(messages)
        + [pl.BlockSpec(memory_space=pl.ANY)] * len(after),
        out_shape=jax.ShapeDtypeStruct(first.shape, BF16),
        compiler_params=params(24),
        cost_estimate=cost(1 * TUNE),
        name="merge_partials",
    )(*messages, *after)


def fold_kernel(start, whole_ref, part_ref, out_ref):
    rows = part_ref.shape[0]
    rest = slice(rows - start, 2 * rows - start)
    out_ref[rest] = whole_ref[rest]
    here = slice(start, start + rows)
    merge_kernel(2, whole_ref.at[here], part_ref, out_ref.at[here])


def fold(whole, part, start):
    return pl.pallas_call(
        functools.partial(fold_kernel, start),
        out_shape=jax.ShapeDtypeStruct(whole.shape, BF16),
        compiler_params=params(24),
        cost_estimate=cost(0.1 * TUNE),
        name="fold_partials",
    )(whole, part)


def outgoing_kernel(prompt_ref, q_ref, out_ref):
    rows, slots = q_ref.shape[0], out_ref.shape[0]
    prompt = prompt_ref[...]
    across = jnp.broadcast_to(prompt, (rows, rows))
    first = lax.broadcasted_iota(jnp.int32, (rows, rows), 0) < lanes((rows, rows))
    earlier = (across.T == across) & first
    arrival = jnp.sum(earlier.astype(jnp.int32), axis=0, keepdims=True)
    slot = lax.broadcasted_iota(jnp.int32, (slots, rows), 0)
    wanted = (slot // (2 * CAP) == prompt) & (slot % CAP == arrival)
    chooser = jnp.where(wanted, 1.0, 0.0).astype(BF16)
    out_ref[...] = jnp.dot(chooser, q_ref[...], preferred_element_type=F32).astype(BF16)


def outgoing_part(row_prompt, queries, slots):
    rows, width = queries.shape
    whole = lambda shape: pl.BlockSpec(shape, lambda i: (0, i))
    return pl.pallas_call(
        outgoing_kernel,
        grid=(4,),
        in_specs=[pl.BlockSpec((1, rows), lambda i: (0, 0)), whole((rows, width // 4))],
        out_specs=whole((slots, width // 4)),
        out_shape=jax.ShapeDtypeStruct((slots, width), BF16),
        compiler_params=params(16),
        name="outgoing_queries",
    )(row_prompt[None, :], queries)


def suffix_kernel(length_ref, slot_ref, q_ref, k_ref, v_ref, mean_ref, stat_ref):
    heads = KEY_HEADS * HEADS_PER_KEY
    rows = q_ref.shape[0]
    shape = (heads, KEY_HEADS * HEAD_WIDTH)
    mine = lanes(shape) // HEAD_WIDTH == lax.broadcasted_iota(jnp.int32, shape, 0) // HEADS_PER_KEY
    square = lanes((heads, 128)) == lax.broadcasted_iota(jnp.int32, (heads, 128), 0)
    for i in range(rows):
        row = pl.program_id(0) * rows + i
        slot = slot_ref[row]
        q = jnp.concatenate([q_ref[i]] * KEY_HEADS, axis=1)
        q = jnp.where(mine, q, jnp.zeros_like(q))
        scores = lax.dot_general(
            q, k_ref[i], (((1,), (1,)), ((), ())), preferred_element_type=F32
        )
        seen = lanes(scores.shape) < length_ref[row]
        scores = jnp.where(seen, scores * SCALE, -jnp.inf)
        top = jnp.max(scores, axis=1, keepdims=True)
        weights = jnp.exp2(scores - top).astype(BF16)
        total = jnp.sum(weights.astype(F32), axis=1, keepdims=True)
        blend = jnp.dot(weights, v_ref[i], preferred_element_type=F32)
        for k in range(KEY_HEADS):
            part = slice(k * HEADS_PER_KEY, (k + 1) * HEADS_PER_KEY)
            mean_ref[slot, part, :] = (
                blend[part, k * HEAD_WIDTH : (k + 1) * HEAD_WIDTH] / total[part]
            )
        level = top + jnp.log2(total)
        stat_ref[slot] = jnp.sum(jnp.where(square, level, 0.0), axis=0, keepdims=True)


def suffix_part(queries, keys, values, length, slot, step=4):
    rows, width = queries.shape
    heads = width // HEAD_WIDTH
    entry = pl.BlockSpec((step,) + keys.shape[1:], lambda r, *_: (r, 0, 0))
    return pl.pallas_call(
        suffix_kernel,
        grid_spec=pltpu.PrefetchScalarGridSpec(
            num_scalar_prefetch=2,
            grid=(rows // step,),
            in_specs=[
                pl.BlockSpec((step, heads, HEAD_WIDTH), lambda r, *_: (r, 0, 0)),
                entry,
                entry,
            ],
            out_specs=[
                pl.BlockSpec((rows, heads, HEAD_WIDTH), lambda r, *_: (0, 0, 0)),
                pl.BlockSpec((rows, 1, 128), lambda r, *_: (0, 0, 0)),
            ],
        ),
        out_shape=[
            jax.ShapeDtypeStruct((rows, heads, HEAD_WIDTH), F32),
            jax.ShapeDtypeStruct((rows, 1, 128), F32),
        ],
        compiler_params=params(58),
        cost_estimate=cost(10),
        name="suffix_attention",
    )(length, slot, queries.reshape(rows, heads, HEAD_WIDTH), keys, values)


def final_kernel(*refs):
    arrived, (pick_ref, mean_ref, stat_ref, out_ref) = refs[:-4], refs[-4:]
    for group, ref in enumerate(arrived):
        width = ref.shape[1] - 128
        count = width // HEAD_WIDTH
        stats, parts = [], []
        for half in range(2):
            chosen = jnp.dot(pick_ref[half], ref[...], preferred_element_type=F32)
            stats.append(decode(chosen[:, width:]))
            parts.append(lambda h, c=chosen: c[:, h * HEAD_WIDTH : (h + 1) * HEAD_WIDTH])
        base = group * width
        stat = stat_ref[:, 0, :]
        if group:
            stat = pltpu.roll(stat, 128 - group * count, 1)
        stats.append(stat)
        parts.append(
            lambda h: mean_ref[:, group * count + h, :]
        )
        out, _ = merged(stats, parts, count)
        for h, x in enumerate(out):
            out_ref[:, base + h * HEAD_WIDTH : base + (h + 1) * HEAD_WIDTH] = x.astype(BF16)


def final_part(arrived, pick, mean, stat):
    return pl.pallas_call(
        final_kernel,
        out_shape=jax.ShapeDtypeStruct((mean.shape[0], mean.shape[1] * mean.shape[2]), BF16),
        compiler_params=params(24),
        name="last_merge",
    )(*arrived, pick, mean, stat)


def swapped(x, turn):
    pairs = {"near": [1, 0, 3, 2], "next": [3, 2, 1, 0], "far": [2, 3, 0, 1]}[turn]
    return lax.ppermute(x, "z", list(enumerate(pairs)))


def in_plane(x):
    return lax.all_to_all(x, ("prefix", "xh"), split_axis=0, concat_axis=0, tiled=True)


def local(
    queries,
    row_prompt,
    suffix_length,
    result_slot,
    prompt_keys,
    prompt_values,
    continuation_keys,
    continuation_values,
):
    sides = lax.axis_size("xh")
    rows = queries.shape[0]
    slots = lax.axis_size("prefix") * sides * CAP
    whole = in_plane(outgoing_part(row_prompt, queries, slots))
    mean, stat = suffix_part(
        queries, continuation_keys, continuation_values, suffix_length, result_slot
    )
    indices = jnp.arange(rows)
    earlier = (row_prompt[:, None] == row_prompt[None, :]) & (indices[None, :] < indices[:, None])
    arrival = jnp.sum(earlier.astype(jnp.int32), axis=1)
    slot = jnp.arange(slots)
    wanted = (slot[None, :] // (sides * CAP) == row_prompt[:, None]) & (
        slot[None, :] % CAP == arrival[:, None]
    )
    placer = indices[:, None] == result_slot[None, :]
    taken = jnp.any(placer[:, :, None] & wanted[None], axis=1)
    side = slot // CAP % sides
    pick = jnp.stack([taken & (side == x)[None] for x in range(2)]).astype(BF16)
    keys, values = prompt_keys[0], prompt_values[0]
    attend = lambda group, queries, after, split=1: prefix_part(
        queries, keys, values, group, after, split
    )
    half, span = slots // 2, queries.shape[1] // GROUPS
    own = [
        [whole[h * half : (h + 1) * half, g * span : (g + 1) * span] for h in range(2)]
        for g in range(GROUPS)
    ]
    near = [[swapped(x, "near") for x in block] for block in own]
    after = [[swapped(x, "next") for x in block] for block in own]
    far = [[swapped(a[0], "near"), swapped(n[1], "next")] for n, a in zip(near, after)]

    def folded(pair, far):
        top, low = swapped(far[0], "near"), swapped(far[1], "next")
        return fold(pair[0], low, half), fold(pair[1], top, 0)

    def back(sent):
        return swapped(sent[0], "near"), swapped(sent[1], "next")

    (own_0,) = attend(0, [own[0]], [stat])
    pair_0 = attend(0, [near[0], after[0]], [own_0])
    far_0 = attend(0, [far[0]], pair_0, 2)
    far_1 = attend(1, [far[1]], far_0, 2)
    sent_0 = folded(pair_0, far_0)
    pair_1 = attend(1, [near[1], after[1]], [*far_1, *sent_0])
    sent_1 = folded(pair_1, far_1)
    (own_1,) = attend(1, [own[1]], sent_1)
    results = [merge([own_0, *back(sent_0)], [own_1]), merge([own_1, *back(sent_1)])]
    returned = in_plane(jnp.concatenate(results, axis=1))
    returned = [returned[:, : span + 128], returned[:, span + 128 :]]
    return final_part(returned, pick, mean, stat)


def solution(mesh):
    fine = Mesh(mesh.devices.reshape(mesh.devices.shape[0], -1, Z), ("prefix", "xh", "z"))
    rows = ("prefix", "xh", "z")
    blocks = ("xh", "z")
    in_specs = (
        P(rows, None),
        P(rows),
        P(rows),
        P(rows),
        P("prefix", blocks, None),
        P("prefix", blocks, None),
        P(rows, None, None),
        P(rows, None, None),
    )
    return jax.shard_map(
        local, mesh=fine, in_specs=in_specs, out_specs=P(rows, None), check_vma=False
    )
```
